32 devices in a mesh: rep: 8 (over z, y), shard: 4 (over x, core).
Axes of the slice: x: 2, y: 2, z: 4, core: 2. Of those that a mesh axis runs over, the one named last changes fastest.
Arguments:
- tokens: bfloat16 [32768, 1024], P(('rep', 'shard')), may hold values from -6 to 6
- lengths: int32 [32, 4], P(('rep', 'shard')), may hold values from 0 to 1024, as said below
- routes: int32 [32768, 8], P(('rep', 'shard')), may hold values from 0 to 15, all different within a row; in each aligned block of 1024 rows (0 to 1023, 1024 to 2047, ...) at most 640 rows name the same one
- w_q: bfloat16 [1024, 1024], P('shard'), may hold values from -0.1875 to 0.1875
- w_kv: bfloat16 [1024, 1024], P('shard'), may hold values from -0.1875 to 0.1875
- w_o: bfloat16 [1024, 1024], P('shard'), may hold values from -0.75 to 0.75
- w_router: bfloat16 [1024, 16], P('shard'), may hold values from -0.09375 to 0.09375
- gain_attn: bfloat16 [1024], P('shard'), may hold values from 0.5 to 1.5
- gain_ffn: bfloat16 [1024], P('shard'), may hold values from 0.5 to 1.5
- w_in: bfloat16 [16, 1024, 1024], P('shard'), may hold values from -0.1875 to 0.1875
- w_out: bfloat16 [16, 512, 1024], P('shard'), may hold values from -1 to 1
- cotangent: bfloat16 [32768, 1024], P(('rep', 'shard')), may hold values from -6 to 6
Outputs:
- out: bfloat16 [32768, 1024], P(('rep', 'shard'))
- d_tokens: bfloat16 [32768, 1024], P(('rep', 'shard'))
- d_w_q: float32 [1024, 1024], P('shard')
- d_w_kv: float32 [1024, 1024], P('shard')
- d_w_o: float32 [1024, 1024], P('shard')
- d_w_router: float32 [1024, 16], P('shard')
- d_gain_attn: float32 [1024], P('shard')
- d_gain_ffn: float32 [1024], P('shard')
- d_w_in: float32 [16, 1024, 1024], P('shard')
- d_w_out: float32 [16, 512, 1024], P('shard')
The draws below stay inside these ranges and needn't reach their ends.
Inputs may be any that keep to these rules, and one draw needn't show every extreme that they name: `lengths`: entry 0 for an unused sequence entry; a pack's sequences, each padded to a multiple of 128 slots, fit its 1024 slots. In every draw some pack holds one sequence of 1024 rows. `routes`: each row names 8 different experts; among the rows of one pack no expert is named more than 640 times, a bound that some block reaches.
All inputs are finite; a program needn't handle non-finite values.
Results may differ from the reference program's by a relative error of at most 0.02.
Values may be sent and summed in bfloat16 or wider, within the bound.
A program may use at most 448 MiB of HBM per device.

```python
import math
import jax
import jax.numpy as jnp
import numpy as np
from jax import lax

D = 1024
HEADS = 16
KV_HEADS = 8
HD = 64
FF = 512
TOP = 8
EXPERTS = 16
TOK_DEV = 1024
BLK = 128
SLOTS = 4
CAP = 640
TOKENS = 32768
N_REP = 8
N_SHARD = 4


def draw_lengths(key, part):
    key = jax.random.fold_in(key, 17)
    device_count = N_REP * N_SHARD
    block_count = TOK_DEV // BLK
    subkeys = jax.random.split(key, 4)
    used_blocks = jax.random.randint(subkeys[0], (device_count, 1), 2, block_count + 1)
    cut_points = jnp.minimum(jax.random.randint(subkeys[1], (device_count, SLOTS - 1), 0, block_count + 1), used_blocks)
    boundaries = jnp.sort(jnp.concatenate([jnp.zeros((device_count, 1), jnp.int32), cut_points, used_blocks], axis=1), axis=1)
    seq_blocks = boundaries[:, 1:] - boundaries[:, :-1]
    tail_rows = jax.random.randint(subkeys[2], (device_count, SLOTS), 1, BLK + 1)
    seq_lens = jnp.where(seq_blocks > 0, (seq_blocks - 1) * BLK + tail_rows, 0)
    full_device = jax.random.randint(subkeys[3], (), 0, device_count)
    full_row = jnp.where(jnp.arange(SLOTS) == 0, TOK_DEV, 0)
    seq_lens = jnp.where(jnp.arange(device_count)[:, None] == full_device, full_row[None, :], seq_lens)
    return seq_lens.astype(jnp.int32)


def block_scale(own_key, shape, pieces, low, largest):
    def one(position, shards_of):
        draws = jax.random.uniform(jax.random.fold_in(jax.random.fold_in(own_key, 6), position), (shards_of,), jnp.float32, low / len(pieces), largest / len(pieces))
        return jnp.repeat(jnp.exp(draws), shape[position] // shards_of).reshape((-1,) + (1,) * (len(shape) - position - 1))

    loudness = one(*pieces[0])
    for cut in pieces[1:]:
        loudness = loudness * one(*cut)
    return loudness


def deal_out(stream_key, own, number, rows, count, top, bound, lean):
    sequence = jax.random.permutation(stream_key, count)
    packed, usual = portions_of(count, rows * top, bound, lean, True), portions_of(count, rows * top, bound, lean, False)
    places = jnp.arange(count)

    def named(sizes, turn):
        used = int((sizes > 0).sum())
        fixed = max(1, used // 4)
        moved = fixed + (places - fixed + turn * (used - fixed)) % max(1, count - fixed)
        return jnp.zeros((count,), jnp.int32).at[sequence[jnp.where(places < fixed, places, moved)]].set(jnp.asarray(sizes, jnp.int32))

    sizes = jnp.where(number % 4 == 0, named(packed, number // 4), named(usual, number - number // 4 - 1))
    mixed = jax.random.permutation(jax.random.fold_in(own, 3), count)
    source_of, receiver = mixed[0:count // 2 * 2:2], mixed[1:count // 2 * 2:2]
    slack = jnp.minimum(sizes[source_of] - 1, bound - sizes[receiver]) // 2
    slack = jnp.where((source_of == sequence[0]) | (receiver == sequence[0]) | (sizes[receiver] == 0), 0, jnp.maximum(slack, 0))
    moved = jax.random.randint(jax.random.fold_in(own, 4), (count // 2,), 0, 1 << 20) % (slack + 1)
    sizes = sizes.at[source_of].add(-moved).at[receiver].add(moved)
    labels = jnp.searchsorted(jnp.cumsum(sizes), jnp.arange(rows * top), side="right").astype(jnp.int32)
    listing = labels.reshape(top, rows).T
    listing = listing[jax.random.permutation(jax.random.fold_in(own, 1), rows)]
    turn = jax.random.randint(jax.random.fold_in(own, 2), (rows, 1), 0, top)
    return jnp.take_along_axis(listing, (jnp.arange(top)[None, :] + turn) % top, axis=1)


def portions_of(count, total, reach, lean, full):
    portions = [(1 << 20) // math.isqrt(rank ** lean) + 1 for rank in range(1, count + 1)]
    largest = reach if full else min(reach, max(-(-total // count), total * portions[0] // sum(portions)))
    least = 1 if total - largest >= count - 1 else 0
    given, rest = [largest] + [least] * (count - 1), total - largest - least * (count - 1)
    while rest > 0:
        free = [i for i in range(1, count) if given[i] < largest] or [i for i in range(1, count) if given[i] < reach]
        whole, budget = sum([portions[i] for i in free]), rest
        for i in free:
            more = min(reach - given[i], max(1, budget * portions[i] // whole), rest)
            given[i] = given[i] + more
            rest = rest - more
    return np.array(given)


def scatter_about(stream_key, extent, width, limit, pieces=(), kind=jnp.bfloat16):
    factor_of = block_scale(stream_key, extent, pieces, -0.22, 0.18) if pieces else 1.0
    array = jax.random.normal(stream_key, extent, jnp.float32) * width * factor_of
    return jnp.minimum(jnp.maximum(array, -limit), limit).astype(kind)


def setup_inputs(seed: int = 0) -> dict:
    keys = jax.random.split(jax.random.key(seed), 13)
    tokens = scatter_about(keys[0], (TOKENS, D), 1.0, 6.0, ((0, 32),))
    lengths = draw_lengths(jax.random.fold_in(keys[12], 71), 0)
    routes_keys = jax.random.split(jax.random.fold_in(keys[2], 1), TOKENS // TOK_DEV)
    routes_turns = jax.random.permutation(jax.random.fold_in(keys[2], 3), TOKENS // TOK_DEV)
    routes = jax.vmap(lambda own, number: deal_out(jax.random.fold_in(keys[2], 2), own, number, TOK_DEV, EXPERTS, TOP, CAP, 1))(routes_keys, routes_turns).reshape((TOKENS, TOP))
    w_q = scatter_about(keys[3], (D, HEADS * HD), D ** -0.5, 0.1875, ((0, 4),))
    w_kv = scatter_about(keys[4], (D, 2 * KV_HEADS * HD), D ** -0.5, 0.1875, ((0, 4),))
    w_o = scatter_about(keys[5], (HEADS * HD, D), (HEADS * HD // 16) ** -0.5, 0.75, ((0, 4),))
    w_router = scatter_about(keys[6], (D, EXPERTS), (4 * D) ** -0.5, 0.09375, ((0, 4),))
    gain_attn = jnp.clip(1.0 + 0.1 * jax.random.normal(keys[7], (D,), jnp.float32), 0.5, 1.5).astype(jnp.bfloat16)
    gain_ffn = jnp.clip(1.0 + 0.1 * jax.random.normal(keys[8], (D,), jnp.float32), 0.5, 1.5).astype(jnp.bfloat16)
    w_in = scatter_about(keys[9], (EXPERTS, D, 2 * FF), D ** -0.5, 0.1875, ((0, 4),))
    w_out = scatter_about(keys[10], (EXPERTS, FF, D), (FF // 16) ** -0.5, 1.0, ((0, 4),))
    cotangent = scatter_about(keys[11], (TOKENS, D), 1.0, 6.0, ((0, 32),))
    return dict(tokens=tokens, lengths=lengths, routes=routes, w_q=w_q, w_kv=w_kv, w_o=w_o, w_router=w_router, gain_attn=gain_attn, gain_ffn=gain_ffn, w_in=w_in, w_out=w_out, cotangent=cotangent)


epsilon = 1e-05
rope_base = 10000.0
neg_fill = -1e+30

@jax.custom_vjp
def low(v):
    return lax.optimization_barrier(v.astype(jnp.bfloat16)).astype(jnp.float32)

@jax.custom_vjp
def low_back(v):
    return v

def low_keep(v):
    return (low(v), None)

def low_pass(kept, grad):
    return (grad,)

def back_keep(v):
    return (v, None)

def back_low(kept, grad):
    return (low(grad),)
low.defvjp(low_keep, low_pass)
low_back.defvjp(back_keep, back_low)

def layout(lengths, tok_rows, block_rows):
    seq_lens = lengths[0].astype(jnp.int32)
    seq_blocks = (seq_lens + block_rows - 1) // block_rows
    seq_starts = (block_rows * (jnp.cumsum(seq_blocks) - seq_blocks)).astype(jnp.int32)
    slot_ids = jnp.arange(tok_rows, dtype=jnp.int32)[:, None]
    member = ((slot_ids >= seq_starts[None, :]) & (slot_ids < seq_starts[None, :] + seq_lens[None, :])).astype(jnp.int32)
    is_valid = lax.optimization_barrier(jnp.sum(member, axis=1)).astype(jnp.int32)
    numbers = jnp.arange(seq_lens.shape[0], dtype=jnp.int32)
    seq_ids = (lax.optimization_barrier(jnp.sum(member * numbers[None, :], axis=1)) + is_valid - 1).astype(jnp.int32)
    places = lax.optimization_barrier(jnp.sum(member * (slot_ids - seq_starts[None, :]), axis=1)).astype(jnp.int32)
    return (is_valid, seq_ids, places)

def rotate(matrix, places, head_count, head_size, direction):
    half_size = head_size // 2
    frequency = rope_base ** (-2.0 * jnp.arange(half_size, dtype=jnp.float32) / head_size)
    angles = places.astype(jnp.float32)[:, None] * frequency[None, :]
    cosine = jnp.cos(angles)[:, None, :]
    sine_part = direction * jnp.sin(angles)[:, None, :]
    shaped = matrix.reshape(matrix.shape[0], head_count, head_size)
    first_half = shaped[:, :, :half_size]
    second_half = shaped[:, :, half_size:]
    turned = jnp.concatenate([first_half * cosine - second_half * sine_part, second_half * cosine + first_half * sine_part], axis=2)
    return turned.reshape(matrix.shape[0], head_count * head_size)

def visible(lead_row, block_rows, is_valid, seq_ids):
    tok_rows = seq_ids.shape[0]
    query_ids = lead_row + jnp.arange(block_rows, dtype=jnp.int32)
    key_ids = jnp.arange(tok_rows, dtype=jnp.int32)
    query_seq = lax.dynamic_slice_in_dim(seq_ids, lead_row, block_rows, 0)
    causal = key_ids[None, :] <= query_ids[:, None]
    same_seq = (query_seq[:, None] == seq_ids[None, :]) & (is_valid[None, :] > 0)
    return same_seq & causal | (key_ids[None, :] == query_ids[:, None])

def attention(q_rot, k_rot, v_val, is_valid, seq_ids):
    block_rows = min(512, TOK_DEV)
    q_group = HEADS // KV_HEADS
    score_scale = HD ** (-0.5)
    q_blocks = q_rot.reshape(TOK_DEV // block_rows, block_rows, KV_HEADS, q_group, HD)
    k_heads = k_rot.reshape(TOK_DEV, KV_HEADS, HD)
    v_heads = v_val.reshape(TOK_DEV, KV_HEADS, HD)
    lead_rows = jnp.arange(TOK_DEV // block_rows, dtype=jnp.int32) * block_rows

    @jax.checkpoint
    def one_block(operands):
        q_rows, lead_row = operands
        raw_scores = jnp.einsum('qhgd,khd->hgqk', q_rows, k_heads, precision=lax.Precision.HIGHEST)
        scores = low_back(raw_scores * score_scale)
        allowed = visible(lead_row, block_rows, is_valid, seq_ids)
        scores = jnp.where(allowed[None, None], scores, neg_fill)
        attn_probs = low(jax.nn.softmax(scores, axis=-1))
        return jnp.einsum('hgqk,khd->qhgd', attn_probs, v_heads, precision=lax.Precision.HIGHEST)
    outputs = lax.map(one_block, (q_blocks, lead_rows))
    return outputs.reshape(TOK_DEV, HEADS * HD)

def dispatch(routes_dev, is_valid):
    expert_ids = jnp.arange(EXPERTS, dtype=jnp.int32)
    chosen = (routes_dev[:, :, None] == expert_ids[None, None, :]).astype(jnp.int32)
    hit_table = lax.optimization_barrier(jnp.sum(chosen, axis=1)) * is_valid[:, None]
    slot_ranks = (jnp.cumsum(hit_table, axis=0) - 1).astype(jnp.int32)
    slot_of = lax.optimization_barrier(jnp.sum(chosen * slot_ranks[:, None, :], axis=2)).astype(jnp.int32)
    sentinel = EXPERTS * CAP
    flat_ids = jnp.where(is_valid[:, None] > 0, routes_dev * CAP + slot_of, sentinel).astype(jnp.int32)
    token_ids = jnp.broadcast_to(jnp.arange(TOK_DEV, dtype=jnp.int32)[:, None], flat_ids.shape)
    slot_source = jnp.full((sentinel + 1,), TOK_DEV, jnp.int32).at[flat_ids.reshape(-1)].set(token_ids.reshape(-1))[:sentinel]
    return (chosen, flat_ids, slot_source)

def device_forward(params, x_dev, lens_dev, routes_dev):
    w_q, w_kv, w_o, w_router, gain_attn, gain_ffn, w_in, w_out = params
    kv_width = KV_HEADS * HD
    is_valid, seq_ids, places = layout(lens_dev[None, :], TOK_DEV, BLK)
    valid_rows = is_valid.astype(jnp.float32)[:, None]
    scale_one = lax.rsqrt(lax.optimization_barrier(jnp.mean(x_dev * x_dev, axis=1, keepdims=True)) + epsilon)
    x_one = low(x_dev * scale_one * gain_attn[None, :])
    q_lin = low_back(jnp.dot(x_one, w_q, precision=lax.Precision.HIGHEST, preferred_element_type=jnp.float32))
    kv_lin = low_back(jnp.dot(x_one, w_kv, precision=lax.Precision.HIGHEST, preferred_element_type=jnp.float32))
    q_rot = low(rotate(q_lin, places, HEADS, HD, 1.0))
    k_rot = low(rotate(kv_lin[:, :kv_width], places, KV_HEADS, HD, 1.0))
    v_val = low(kv_lin[:, kv_width:])
    attended = low(low_back(attention(q_rot, k_rot, v_val, is_valid, seq_ids)))
    branch = low_back(jnp.dot(attended, w_o, precision=lax.Precision.HIGHEST, preferred_element_type=jnp.float32))
    mixed_rows = x_dev + valid_rows * branch
    scale_two = lax.rsqrt(lax.optimization_barrier(jnp.mean(mixed_rows * mixed_rows, axis=1, keepdims=True)) + epsilon)
    x_two = low(mixed_rows * scale_two * gain_ffn[None, :])
    logits = low_back(jnp.dot(x_two, w_router, precision=lax.Precision.HIGHEST, preferred_element_type=jnp.float32))
    chosen, flat_ids, slot_source = dispatch(routes_dev, is_valid)
    picked = lax.optimization_barrier(jnp.sum(chosen.astype(jnp.float32) * logits[:, None, :], axis=2))
    gate_probs = jax.nn.softmax(picked, axis=1)
    x_pad = jnp.concatenate([x_two, jnp.zeros((1, D), jnp.float32)], axis=0)
    inputs = low_back(x_pad[slot_source].reshape(EXPERTS, CAP, D))
    both_lin = low_back(jnp.einsum('ecd,edf->ecf', inputs, w_in, precision=lax.Precision.HIGHEST))
    hidden = low(jax.nn.silu(both_lin[:, :, :FF]) * both_lin[:, :, FF:])
    result = low(low_back(jnp.einsum('ecf,efd->ecd', hidden, w_out, precision=lax.Precision.HIGHEST)))
    result_pad = jnp.concatenate([result.reshape(EXPERTS * CAP, D), jnp.zeros((1, D), jnp.float32)], axis=0)
    mixture = jnp.zeros_like(mixed_rows)
    for column in range(TOP):
        mixture = mixture + gate_probs[:, column:column + 1] * result_pad[flat_ids[:, column]]
    return mixed_rows + mixture

def reference(tokens, lengths, routes, w_q, w_kv, w_o, w_router, gain_attn, gain_ffn, w_in, w_out, cotangent):
    device_count = N_REP * N_SHARD
    params = tuple((weight.astype(jnp.float32) for weight in (w_q, w_kv, w_o, w_router, gain_attn, gain_ffn, w_in, w_out)))
    x_all = tokens.astype(jnp.float32).reshape(device_count, TOK_DEV, D)
    routes_all = routes.reshape(device_count, TOK_DEV, TOP)
    checked = jax.checkpoint(device_forward)

    def forward(weights, inputs):

        def device_step(state_none, operands):
            x_dev, lens_dev, routes_dev = operands
            return (state_none, checked(weights, x_dev, lens_dev, routes_dev))
        unused, outputs = lax.scan(device_step, None, (inputs, lengths, routes_all))
        return outputs
    outputs, pullback = jax.vjp(forward, params, x_all)
    gradients, d_inputs = pullback(cotangent.astype(jnp.float32).reshape(device_count, TOK_DEV, D))
    return (outputs.reshape(-1, D).astype(jnp.bfloat16), d_inputs.reshape(-1, D).astype(jnp.bfloat16), gradients[0], gradients[1], gradients[2], gradients[3], gradients[4], gradients[5], gradients[6], gradients[7])
```

```python
import functools

import jax
import jax.numpy as jnp
from jax import lax
from jax.experimental import pallas as pl
from jax.experimental.pallas import tpu as pltpu
from jax.sharding import PartitionSpec as P

HEADS = 16
KV_HEADS = 8
HD = 64
FF = 512
TOP = 8
EXPERTS = 16
BLK = 128


epsilon = 1e-05
rope_base = 10000.0
neg_fill = -1e30


def layout(lengths, tok_rows, block_rows):
    seq_lens = lengths[0]
    seq_blocks = (seq_lens + block_rows - 1) // block_rows
    seq_starts = block_rows * (jnp.cumsum(seq_blocks) - seq_blocks)
    slot_ids = jnp.arange(tok_rows, dtype=jnp.int32)[:, None]
    member = (
        (slot_ids >= seq_starts[None, :]) & (slot_ids < seq_starts[None, :] + seq_lens[None, :])
    ).astype(jnp.int32)
    is_valid = jnp.sum(member, axis=1)
    numbers = jnp.arange(seq_lens.shape[0], dtype=jnp.int32)
    seq_ids = jnp.sum(member * numbers[None, :], axis=1) + is_valid - 1
    places = jnp.sum(member * (slot_ids - seq_starts[None, :]), axis=1)
    return (is_valid, seq_ids, places)


def rotate(matrix, places, head_count, head_size, direction):
    half_size = head_size // 2
    frequency = rope_base ** (-2.0 * jnp.arange(half_size, dtype=jnp.float32) / head_size)
    angles = places.astype(jnp.float32)[:, None] * frequency[None, :]
    cosine = jnp.cos(angles)[:, None, :]
    sine_part = direction * jnp.sin(angles)[:, None, :]
    shaped = matrix.reshape(matrix.shape[0], head_count, head_size)
    first_half = shaped[:, :, :half_size]
    second_half = shaped[:, :, half_size:]
    turned = jnp.concatenate(
        [
            first_half * cosine - second_half * sine_part,
            second_half * cosine + first_half * sine_part,
        ],
        axis=2,
    )
    return turned.reshape(matrix.shape[0], head_count * head_size)


NN = (((1,), (0,)), ((), ()))
NT = (((1,), (1,)), ((), ()))
TN = (((0,), (0,)), ((), ()))
QB = 256


def mm(a, b, dims):
    return lax.dot_general(a, b, dims, preferred_element_type=jnp.float32)


def block_mask(qseq_ref, kseq_ref, lo, hi):
    rows = lo + lax.broadcasted_iota(jnp.int32, (hi - lo, hi), 0)
    cols = lax.broadcasted_iota(jnp.int32, (hi - lo, hi), 1)
    qs = qseq_ref[lo:hi, :]
    ks = kseq_ref[:, 0:hi]
    return ((qs == ks) & (ks >= 0) & (cols <= rows)) | (cols == rows)


def row_probs(q, k, allowed):
    scores = jnp.where(allowed, mm(q, k, NT) * (HD ** (-0.5)), neg_fill)
    shifted = jnp.exp(scores - jnp.max(scores, axis=1, keepdims=True))
    return shifted * (1.0 / jnp.sum(shifted, axis=1, keepdims=True))


def attend_fwd_kernel(qseq_ref, kseq_ref, q_ref, k_ref, v_ref, o_ref):
    rows = q_ref.shape[0]
    step = min(QB, rows)
    for lo in range(0, rows, step):
        hi = lo + step
        allowed = block_mask(qseq_ref, kseq_ref, lo, hi)
        outs = []
        for head in range(4):
            kv = head // 2
            q = q_ref[lo:hi, head * HD : (head + 1) * HD]
            k = k_ref[0:hi, kv * HD : (kv + 1) * HD]
            v = v_ref[0:hi, kv * HD : (kv + 1) * HD]
            probs = row_probs(q, k, allowed).astype(jnp.bfloat16)
            outs.append(mm(probs, v, NN))
        o_ref[lo:hi, :] = jnp.concatenate(outs, axis=1).astype(jnp.bfloat16)


def attend_bwd_kernel(qseq_ref, kseq_ref, q_ref, k_ref, v_ref, d_ref, dq_ref, dk_ref, dv_ref):
    rows = q_ref.shape[0]
    step = min(QB, rows)
    scale = HD ** (-0.5)
    dk_ref[...] = jnp.zeros_like(dk_ref)
    dv_ref[...] = jnp.zeros_like(dv_ref)
    for lo in range(0, rows, step):
        hi = lo + step
        allowed = block_mask(qseq_ref, kseq_ref, lo, hi)
        dqs = []
        dks = []
        dvs = []
        for kv in range(2):
            k = k_ref[0:hi, kv * HD : (kv + 1) * HD]
            v = v_ref[0:hi, kv * HD : (kv + 1) * HD]
            dk = None
            dv = None
            for head in (2 * kv, 2 * kv + 1):
                q = q_ref[lo:hi, head * HD : (head + 1) * HD]
                d = d_ref[lo:hi, head * HD : (head + 1) * HD]
                probs = row_probs(q, k, allowed)
                d_probs = mm(d, v, NT)
                inner = jnp.sum(probs * d_probs, axis=1, keepdims=True)
                d_scores = (probs * (d_probs - inner)).astype(jnp.bfloat16)
                dqs.append(mm(d_scores, k, NN) * scale)
                dk_one = mm(d_scores, q, TN) * scale
                dv_one = mm(probs.astype(jnp.bfloat16), d, TN)
                dk = dk_one if dk is None else dk + dk_one
                dv = dv_one if dv is None else dv + dv_one
            dks.append(dk)
            dvs.append(dv)
        dq_ref[lo:hi, :] = jnp.concatenate(dqs, axis=1)
        dk_ref[0:hi, :] += jnp.concatenate(dks, axis=1)
        dv_ref[0:hi, :] += jnp.concatenate(dvs, axis=1)


def attend_specs(rows):
    return (
        pl.BlockSpec((rows, 1), lambda h: (0, 0)),
        pl.BlockSpec((1, rows), lambda h: (0, 0)),
        pl.BlockSpec((rows, 4 * HD), lambda h: (0, h)),
        pl.BlockSpec((rows, 2 * HD), lambda h: (0, h)),
        pl.BlockSpec((rows, 2 * HD), lambda h: (0, h)),
    )


def attend_forward(q_rot, k_rot, v_val, key_seq):
    rows = q_rot.shape[0]
    specs = attend_specs(rows)
    return pl.pallas_call(
        attend_fwd_kernel,
        grid=(KV_HEADS // 2,),
        in_specs=list(specs),
        out_specs=specs[2],
        out_shape=jax.ShapeDtypeStruct(q_rot.shape, jnp.bfloat16),
        compiler_params=pltpu.CompilerParams(vmem_limit_bytes=48 * 2**20),
        cost_estimate=pl.CostEstimate(
            flops=16 * HEADS * rows * rows * HD, bytes_accessed=8 * 2**20, transcendentals=0
        ),
    )(key_seq[:, None], key_seq[None, :], q_rot, k_rot, v_val)


def attend_backward(q_rot, k_rot, v_val, d_attended, key_seq):
    rows = q_rot.shape[0]
    specs = attend_specs(rows)
    return pl.pallas_call(
        attend_bwd_kernel,
        grid=(KV_HEADS // 2,),
        in_specs=list(specs) + [specs[2]],
        out_specs=[specs[2], specs[3], specs[4]],
        out_shape=[
            jax.ShapeDtypeStruct(q_rot.shape, jnp.float32),
            jax.ShapeDtypeStruct(k_rot.shape, jnp.float32),
            jax.ShapeDtypeStruct(k_rot.shape, jnp.float32),
        ],
        compiler_params=pltpu.CompilerParams(vmem_limit_bytes=48 * 2**20),
        cost_estimate=pl.CostEstimate(
            flops=40 * HEADS * rows * rows * HD, bytes_accessed=20 * 2**20, transcendentals=0
        ),
    )(key_seq[:, None], key_seq[None, :], q_rot, k_rot, v_val, d_attended)


def expert_kernel(
    lead_ref, x_ref, xt_ref, g_ref, gates_ref, win_ref, wout_ref, mix_in, dx_in,
    mix_ref, dx_ref, dg_ref, dwin_ref, dwout_ref, gh_ref, dgu_ref,
):
    step = pl.program_id(0)

    @pl.when(step == 0)
    def _():
        mix_ref[...] = mix_in[...]
        dx_ref[...] = dx_in[...]
        dg_ref[...] = jnp.zeros_like(dg_ref)

    expert = lead_ref[0] + step
    rows = x_ref.shape[0]
    chunk = min(256, rows)
    for lo in range(0, rows, chunk):
        part = slice(lo, lo + chunk)
        gates = gates_ref[part, :]
        lane = lax.broadcasted_iota(jnp.int32, gates.shape, 1) == expert
        gate = jnp.sum(jnp.where(lane, gates, 0.0), axis=1, keepdims=True)
        both = mm(x_ref[part, :], win_ref[0], NN)
        dh0 = mm(g_ref[part, :], wout_ref[0], NT)
        a = both[:, :FF]
        up = both[:, FF:]
        s = 1.0 / (1.0 + jnp.exp(-a))
        act = a * s
        hid = act * up
        dgate = jnp.sum(hid * dh0, axis=1, keepdims=True)
        dg_ref[part, :] += jnp.where(lane, dgate, 0.0)
        gh = (gate * hid).astype(jnp.bfloat16)
        gh_ref[part, :] = gh
        mix_ref[part, :] += mm(gh, wout_ref[0], NN)
        dh = gate * dh0
        dgu_ref[part, :FF] = (dh * up * (s * (1.0 + a * (1.0 - s)))).astype(jnp.bfloat16)
        dgu_ref[part, FF:] = (dh * act).astype(jnp.bfloat16)
        dx_ref[part, :] += mm(dgu_ref[part, :], win_ref[0], NT)
    width = xt_ref.shape[0]
    for lo in range(0, width, 256):
        part = slice(lo, lo + 256)
        dwin_ref[0, part, :] = mm(xt_ref[part, :], dgu_ref[...], NN).astype(jnp.bfloat16)
    for lo in range(0, FF, 256):
        part = slice(lo, lo + 256)
        dwout_ref[0, part, :] = mm(gh_ref[:, part], g_ref[...], TN).astype(jnp.bfloat16)


def expert_call(lead, x_two, x_turned, cotangent, gates, w_in, w_out, mix, dx):
    rows, width = x_two.shape
    count = w_in.shape[0]
    one = pl.Buffered(1)

    def whole(shape):
        return pl.BlockSpec(shape, lambda e, lead_ref: (0, 0), pipeline_mode=one)

    win_spec = pl.BlockSpec((1,) + w_in.shape[1:], lambda e, lead_ref: (e, 0, 0))
    wout_spec = pl.BlockSpec((1,) + w_out.shape[1:], lambda e, lead_ref: (e, 0, 0))
    full = whole((rows, width))
    return pl.pallas_call(
        expert_kernel,
        grid_spec=pltpu.PrefetchScalarGridSpec(
            num_scalar_prefetch=1,
            grid=(count,),
            in_specs=[
                full, whole((width, rows)), full, whole(gates.shape), win_spec, wout_spec, full, full
            ],
            out_specs=[full, full, whole(gates.shape), win_spec, wout_spec],
            scratch_shapes=[
                pltpu.VMEM((rows, FF), jnp.bfloat16),
                pltpu.VMEM((rows, 2 * FF), jnp.bfloat16),
            ],
        ),
        out_shape=[
            jax.ShapeDtypeStruct(mix.shape, jnp.float32),
            jax.ShapeDtypeStruct(dx.shape, jnp.float32),
            jax.ShapeDtypeStruct(gates.shape, jnp.float32),
            jax.ShapeDtypeStruct(w_in.shape, jnp.bfloat16),
            jax.ShapeDtypeStruct(w_out.shape, jnp.bfloat16),
        ],
        input_output_aliases={7: 0, 8: 1},
        compiler_params=pltpu.CompilerParams(vmem_limit_bytes=58 * 2**20),
        cost_estimate=pl.CostEstimate(
            flops=count * 18 * rows * width * FF,
            bytes_accessed=count * 12 * 2**20 + 24 * 2**20,
            transcendentals=0,
        ),
    )(lead, x_two, x_turned, cotangent, gates, w_in, w_out, mix, dx)


def swap(array, axis, size, bit):
    return lax.ppermute(array, axis, [(i, i ^ bit) for i in range(size)])


def bits_of(size):
    return [1 << b for b in range(size.bit_length() - 1)]


def spread(own, size):
    slots = [own]
    for j in range(1, size):
        low = j & -j
        slots.append(None)
    for bit in reversed(bits_of(size)):
        for j in range(0, size, 2 * bit):
            slots[j + bit] = swap(slots[j], "shard", size, bit)
    return slots


def fold(slots, size):
    slots = list(slots)
    for bit in bits_of(size):
        for j in range(0, size, 2 * bit):
            slots[j] = slots[j] + swap(slots[j + bit], "shard", size, bit)
    return slots[0]


def sum_rep(piece, size):
    me = lax.axis_index("rep")
    for bit in bits_of(size):
        half = piece.shape[0] // 2
        side = (me // bit) % 2
        keep = lax.dynamic_slice_in_dim(piece, side * half, half, 0)
        give = lax.dynamic_slice_in_dim(piece, (1 - side) * half, half, 0)
        piece = keep + swap(give, "rep", size, bit)
    for bit in reversed(bits_of(size)):
        side = (me // bit) % 2
        other = swap(piece, "rep", size, bit)
        first = jnp.where(side == 0, piece, other)
        second = jnp.where(side == 0, other, piece)
        piece = jnp.concatenate([first, second], axis=0)
    return piece


def pack(parts, multiple):
    wide = parts[0].shape[1]
    rows = [parts[0]]
    small = jnp.concatenate([p.reshape(-1) for p in parts[1:]])
    count = -(-small.shape[0] // wide)
    total = -(-(parts[0].shape[0] + count) // multiple) * multiple - parts[0].shape[0]
    small = jnp.pad(small, (0, total * wide - small.shape[0])).reshape(total, wide)
    return jnp.concatenate([parts[0], small], axis=0)


def owned(array, size, slot):
    rows = array.shape[0] // size
    lead = (lax.axis_index("shard") ^ slot) * rows
    return lax.dynamic_slice_in_dim(array, lead, rows, 0).astype(jnp.bfloat16)


def norm_back(d_normed, normed, gain_vec, inverse_rms):
    scaled = d_normed * gain_vec
    return inverse_rms * (scaled - normed * jnp.mean(scaled * normed, axis=1, keepdims=True))


def local(
    n_rep, n_shard,
    tokens, lengths, routes, w_q, w_kv, w_o, w_router, gain_attn, gain_ffn, w_in, w_out, cotangent,
):
    tok_rows = tokens.shape[0]
    kv_width = KV_HEADS * HD
    expert_count = w_in.shape[0] * n_shard
    per_dev = w_in.shape[0]
    is_valid, seq_ids, places = layout(lengths, tok_rows, BLK)
    valid_rows = is_valid.astype(jnp.float32)[:, None]
    key_seq = jnp.where(is_valid > 0, seq_ids, -1)
    q_full, kv_full, o_full, router_full, gain_one, gain_two = (
        lax.all_gather(w_q, "shard", axis=0, tiled=True),
        lax.all_gather(w_kv, "shard", axis=0, tiled=True),
        lax.all_gather(w_o, "shard", axis=0, tiled=True),
        lax.all_gather(w_router, "shard", axis=0, tiled=True),
        lax.all_gather(gain_attn, "shard", axis=0, tiled=True),
        lax.all_gather(gain_ffn, "shard", axis=0, tiled=True),
    )
    gain_one = gain_one.astype(jnp.float32)[None, :]
    gain_two = gain_two.astype(jnp.float32)[None, :]
    win_slots = spread(w_in, n_shard)
    wout_slots = spread(w_out, n_shard)
    x_float = tokens.astype(jnp.float32)
    scale_one = lax.rsqrt(jnp.mean(x_float * x_float, axis=1, keepdims=True) + epsilon)
    normed_one = x_float * scale_one
    x_one = (normed_one * gain_one).astype(jnp.bfloat16)
    q_lin = jnp.dot(x_one, q_full, preferred_element_type=jnp.float32)
    kv_lin = jnp.dot(x_one, kv_full, preferred_element_type=jnp.float32)
    q_rot = rotate(q_lin, places, HEADS, HD, 1.0).astype(jnp.bfloat16)
    k_rot = rotate(kv_lin[:, :kv_width], places, KV_HEADS, HD, 1.0).astype(jnp.bfloat16)
    v_val = kv_lin[:, kv_width:].astype(jnp.bfloat16)
    attended = attend_forward(q_rot, k_rot, v_val, key_seq)
    branch = jnp.dot(attended, o_full, preferred_element_type=jnp.float32)
    mixed_rows = x_float + valid_rows * branch
    scale_two = lax.rsqrt(jnp.mean(mixed_rows * mixed_rows, axis=1, keepdims=True) + epsilon)
    normed_two = mixed_rows * scale_two
    x_two = (normed_two * gain_two).astype(jnp.bfloat16)
    logits = jnp.dot(x_two, router_full, preferred_element_type=jnp.float32)
    expert_ids = jnp.arange(expert_count, dtype=jnp.int32)
    named = jnp.any(routes[:, :, None] == expert_ids[None, None, :], axis=1)
    top_logit = jnp.max(jnp.where(named, logits, -jnp.inf), axis=1, keepdims=True)
    raised = jnp.where(named, jnp.exp(jnp.where(named, logits - top_logit, 0.0)), 0.0)
    gates = valid_rows * (raised / jnp.sum(raised, axis=1, keepdims=True))
    x_turned = x_two.T
    me = lax.axis_index("shard")
    mix = mixed_rows
    dx = jnp.zeros_like(mixed_rows)
    d_gates = jnp.zeros_like(gates)
    gin_slots = [None] * n_shard
    gout_slots = [None] * n_shard
    for j in range(n_shard):
        lead = ((me ^ j) * per_dev).astype(jnp.int32).reshape(1)
        mix, dx, d_part, gin_slots[j], gout_slots[j] = expert_call(
            lead, x_two, x_turned, cotangent, gates, win_slots[j], wout_slots[j], mix, dx
        )
        d_gates = d_gates + d_part
    layer_out = mix.astype(jnp.bfloat16)
    pieces = []
    low = 1
    gin_fold = list(gin_slots)
    gout_fold = list(gout_slots)
    for j in range(0, n_shard, 2):
        moved_in = swap(gin_slots[j + 1], "shard", n_shard, low)
        moved_out = swap(gout_slots[j + 1], "shard", n_shard, low)
        gin_fold[j] = (gin_slots[j], moved_in)
        gout_fold[j] = (gout_slots[j], moved_out)
    for e in range(per_dev):
        slots = [
            jnp.concatenate(
                [
                    gin_fold[j][0][e] + gin_fold[j][1][e],
                    gout_fold[j][0][e] + gout_fold[j][1][e],
                ],
                axis=0,
            )
            for j in range(0, n_shard, 2)
        ]
        for bit in bits_of(n_shard // 2):
            for j in range(0, n_shard // 2, 2 * bit):
                slots[j] = slots[j] + swap(slots[j + bit], "shard", n_shard, 2 * bit)
        pieces.append(sum_rep(slots[0], n_rep))
    width = w_in.shape[1]
    grad_in = jnp.stack([piece[:width] for piece in pieces]).astype(jnp.float32)
    grad_out = jnp.stack([piece[width:] for piece in pieces]).astype(jnp.float32)

    d_out = cotangent.astype(jnp.float32)
    d_logits = (gates * (d_gates - jnp.sum(gates * d_gates, axis=1, keepdims=True))).astype(
        jnp.bfloat16
    )
    d_router = jnp.einsum("td,te->de", x_two, d_logits, preferred_element_type=jnp.float32)
    d_two = dx + jnp.einsum("te,de->td", d_logits, router_full, preferred_element_type=jnp.float32)
    d_gain_two = jnp.sum(d_two * normed_two, axis=0)
    d_mixed = d_out + norm_back(d_two, normed_two, gain_two, scale_two)
    d_branch = (valid_rows * d_mixed).astype(jnp.bfloat16)
    d_w_o = jnp.einsum("tq,td->qd", attended, d_branch, preferred_element_type=jnp.float32)
    d_attended = jnp.einsum(
        "td,qd->tq", d_branch, o_full, preferred_element_type=jnp.float32
    ).astype(jnp.bfloat16)
    early = sum_rep(
        fold(
            [
                pack(
                    [
                        owned(d_w_o, n_shard, j),
                        owned(d_router, n_shard, j),
                        owned(d_gain_two, n_shard, j),
                    ],
                    16 * n_rep,
                )
                for j in range(n_shard)
            ],
            n_shard,
        ),
        n_rep,
    )
    d_query, d_keys, d_vals = attend_backward(q_rot, k_rot, v_val, d_attended, key_seq)
    d_q_lin = rotate(d_query, places, HEADS, HD, -1.0).astype(jnp.bfloat16)
    d_kv_lin = jnp.concatenate([rotate(d_keys, places, KV_HEADS, HD, -1.0), d_vals], axis=1).astype(
        jnp.bfloat16
    )
    d_w_q = jnp.einsum("td,tq->dq", x_one, d_q_lin, preferred_element_type=jnp.float32)
    d_w_kv = jnp.einsum("td,tq->dq", x_one, d_kv_lin, preferred_element_type=jnp.float32)
    d_one = jnp.einsum(
        "tq,dq->td", d_q_lin, q_full, preferred_element_type=jnp.float32
    ) + jnp.einsum("tq,dq->td", d_kv_lin, kv_full, preferred_element_type=jnp.float32)
    d_gain_one = jnp.sum(d_one * normed_one, axis=0)
    d_tokens = (d_mixed + norm_back(d_one, normed_one, gain_one, scale_one)).astype(jnp.bfloat16)
    late = sum_rep(
        fold(
            [
                pack(
                    [
                        jnp.concatenate([owned(d_w_q, n_shard, j), owned(d_w_kv, n_shard, j)], axis=0),
                        owned(d_gain_one, n_shard, j),
                    ],
                    16,
                )
                for j in range(n_shard)
            ],
            n_shard,
        ),
        n_rep,
    )
    own_rows = w_q.shape[0]
    small = early[own_rows:].reshape(-1).astype(jnp.float32)
    router_size = own_rows * expert_count
    return (
        layer_out,
        d_tokens,
        late[:own_rows].astype(jnp.float32),
        late[own_rows : 2 * own_rows].astype(jnp.float32),
        early[:own_rows].astype(jnp.float32),
        small[:router_size].reshape(own_rows, expert_count),
        late[2 * own_rows :].reshape(-1)[:own_rows].astype(jnp.float32),
        small[router_size : router_size + own_rows],
        grad_in,
        grad_out,
    )


def solution(mesh):
    placed = (
        P(("rep", "shard"), None),
        P(("rep", "shard"), None),
        P(("rep", "shard"), None),
        P("shard", None),
        P("shard", None),
        P("shard", None),
        P("shard", None),
        P("shard"),
        P("shard"),
        P("shard", None, None),
        P("shard", None, None),
        P(("rep", "shard"), None),
    )
    return jax.shard_map(
        functools.partial(local, mesh.shape["rep"], mesh.shape["shard"]),
        mesh=mesh,
        in_specs=placed,
        out_specs=(
            P(("rep", "shard"), None),
            P(("rep", "shard"), None),
            P("shard", None),
            P("shard", None),
            P("shard", None),
            P("shard", None),
            P("shard"),
            P("shard"),
            P("shard", None, None),
            P("shard", None, None),
        ),
        check_vma=False,
    )
```

```python
import functools

import jax
import jax.numpy as jnp
from jax import lax
from jax.experimental import pallas as pl
from jax.experimental.pallas import tpu as pltpu
from jax.sharding import PartitionSpec as P

HEADS = 16
KV_HEADS = 8
HD = 64
FF = 512
TOP = 8
EXPERTS = 16
BLK = 128


epsilon = 1e-05
rope_base = 10000.0
neg_fill = -1e30


def layout(lengths, tok_rows, block_rows):
    seq_lens = lengths[0]
    seq_blocks = (seq_lens + block_rows - 1) // block_rows
    seq_starts = block_rows * (jnp.cumsum(seq_blocks) - seq_blocks)
    slot_ids = jnp.arange(tok_rows, dtype=jnp.int32)[:, None]
    member = (
        (slot_ids >= seq_starts[None, :]) & (slot_ids < seq_starts[None, :] + seq_lens[None, :])
    ).astype(jnp.int32)
    is_valid = jnp.sum(member, axis=1)
    numbers = jnp.arange(seq_lens.shape[0], dtype=jnp.int32)
    seq_ids = jnp.sum(member * numbers[None, :], axis=1) + is_valid - 1
    places = jnp.sum(member * (slot_ids - seq_starts[None, :]), axis=1)
    return (is_valid, seq_ids, places)


def rotate(matrix, places, head_count, head_size, direction):
    half_size = head_size // 2
    frequency = rope_base ** (-2.0 * jnp.arange(half_size, dtype=jnp.float32) / head_size)
    angles = places.astype(jnp.float32)[:, None] * frequency[None, :]
    cosine = jnp.cos(angles)[:, None, :]
    sine_part = direction * jnp.sin(angles)[:, None, :]
    shaped = matrix.reshape(matrix.shape[0], head_count, head_size)
    first_half = shaped[:, :, :half_size]
    second_half = shaped[:, :, half_size:]
    turned = jnp.concatenate(
        [
            first_half * cosine - second_half * sine_part,
            second_half * cosine + first_half * sine_part,
        ],
        axis=2,
    )
    return turned.reshape(matrix.shape[0], head_count * head_size)


NN = (((1,), (0,)), ((), ()))
NT = (((1,), (1,)), ((), ()))
TN = (((0,), (0,)), ((), ()))
QB = 256


def mm(a, b, dims):
    return lax.dot_general(a, b, dims, preferred_element_type=jnp.float32)


def block_mask(qseq_ref, kseq_ref, lo, hi):
    rows = lo + lax.broadcasted_iota(jnp.int32, (hi - lo, hi), 0)
    cols = lax.broadcasted_iota(jnp.int32, (hi - lo, hi), 1)
    qs = qseq_ref[lo:hi, :]
    ks = kseq_ref[:, 0:hi]
    return ((qs == ks) & (ks >= 0) & (cols <= rows)) | (cols == rows)


def row_probs(q, k, allowed):
    scores = jnp.where(allowed, mm(q, k, NT) * (HD ** (-0.5)), neg_fill)
    shifted = jnp.exp(scores - jnp.max(scores, axis=1, keepdims=True))
    return shifted * (1.0 / jnp.sum(shifted, axis=1, keepdims=True))


def attend_fwd_kernel(qseq_ref, kseq_ref, q_ref, k_ref, v_ref, o_ref):
    rows = q_ref.shape[0]
    step = min(QB, rows)
    for lo in range(0, rows, step):
        hi = lo + step
        allowed = block_mask(qseq_ref, kseq_ref, lo, hi)
        outs = []
        for head in range(4):
            kv = head // 2
            q = q_ref[lo:hi, head * HD : (head + 1) * HD]
            k = k_ref[0:hi, kv * HD : (kv + 1) * HD]
            v = v_ref[0:hi, kv * HD : (kv + 1) * HD]
            probs = row_probs(q, k, allowed).astype(jnp.bfloat16)
            outs.append(mm(probs, v, NN))
        o_ref[lo:hi, :] = jnp.concatenate(outs, axis=1).astype(jnp.bfloat16)


def attend_bwd_kernel(
    qseq_ref, kseq_ref, q_ref, k_ref, v_ref, d_ref, held_ref, dq_ref, dk_ref, dv_ref
):
    rows = q_ref.shape[0]
    step = min(QB, rows)
    scale = HD ** (-0.5)
    dk_ref[...] = jnp.zeros_like(dk_ref)
    dv_ref[...] = jnp.zeros_like(dv_ref)
    for lo in range(0, rows, step):
        hi = lo + step
        allowed = block_mask(qseq_ref, kseq_ref, lo, hi)
        dqs = []
        dks = []
        dvs = []
        for kv in range(2):
            k = k_ref[0:hi, kv * HD : (kv + 1) * HD]
            v = v_ref[0:hi, kv * HD : (kv + 1) * HD]
            dk = None
            dv = None
            for head in (2 * kv, 2 * kv + 1):
                q = q_ref[lo:hi, head * HD : (head + 1) * HD]
                d = d_ref[lo:hi, head * HD : (head + 1) * HD]
                probs = row_probs(q, k, allowed)
                d_probs = mm(d, v, NT)
                inner = jnp.sum(probs * d_probs, axis=1, keepdims=True)
                d_scores = (probs * (d_probs - inner)).astype(jnp.bfloat16)
                dqs.append(mm(d_scores, k, NN) * scale)
                dk_one = mm(d_scores, q, TN) * scale
                dv_one = mm(probs.astype(jnp.bfloat16), d, TN)
                dk = dk_one if dk is None else dk + dk_one
                dv = dv_one if dv is None else dv + dv_one
            dks.append(dk)
            dvs.append(dv)
        dq_ref[lo:hi, :] = jnp.concatenate(dqs, axis=1)
        dk_ref[0:hi, :] += jnp.concatenate(dks, axis=1)
        dv_ref[0:hi, :] += jnp.concatenate(dvs, axis=1)


def attend_specs(rows):
    return (
        pl.BlockSpec((rows, 1), lambda h: (0, 0)),
        pl.BlockSpec((1, rows), lambda h: (0, 0)),
        pl.BlockSpec((rows, 4 * HD), lambda h: (0, h)),
        pl.BlockSpec((rows, 2 * HD), lambda h: (0, h)),
        pl.BlockSpec((rows, 2 * HD), lambda h: (0, h)),
    )


def attend_forward(q_rot, k_rot, v_val, key_seq):
    rows = q_rot.shape[0]
    specs = attend_specs(rows)
    return pl.pallas_call(
        attend_fwd_kernel,
        grid=(KV_HEADS // 2,),
        in_specs=list(specs),
        out_specs=specs[2],
        out_shape=jax.ShapeDtypeStruct(q_rot.shape, jnp.bfloat16),
        compiler_params=pltpu.CompilerParams(vmem_limit_bytes=48 * 2**20),
        cost_estimate=pl.CostEstimate(
            flops=16 * HEADS * rows * rows * HD, bytes_accessed=8 * 2**20, transcendentals=0
        ),
    )(key_seq[:, None], key_seq[None, :], q_rot, k_rot, v_val)


def attend_backward(q_rot, k_rot, v_val, d_attended, key_seq, held):
    rows = q_rot.shape[0]
    specs = attend_specs(rows)
    return pl.pallas_call(
        attend_bwd_kernel,
        grid=(KV_HEADS // 2,),
        in_specs=list(specs) + [specs[2], pl.BlockSpec(memory_space=pl.ANY)],
        out_specs=[specs[2], specs[3], specs[4]],
        out_shape=[
            jax.ShapeDtypeStruct(q_rot.shape, jnp.float32),
            jax.ShapeDtypeStruct(k_rot.shape, jnp.float32),
            jax.ShapeDtypeStruct(k_rot.shape, jnp.float32),
        ],
        compiler_params=pltpu.CompilerParams(vmem_limit_bytes=48 * 2**20),
        cost_estimate=pl.CostEstimate(
            flops=40 * HEADS * rows * rows * HD, bytes_accessed=20 * 2**20, transcendentals=0
        ),
    )(key_seq[:, None], key_seq[None, :], q_rot, k_rot, v_val, d_attended, held)


def expert_kernel(
    lead_ref, x_ref, xt_ref, g_ref, gates_ref, win_ref, wout_ref, mix_in, dx_in,
    mix_ref, dx_ref, dg_ref, dwin_ref, dwout_ref, gh_ref, dgu_ref,
):
    step = pl.program_id(0)

    @pl.when(step == 0)
    def _():
        mix_ref[...] = mix_in[...]
        dx_ref[...] = dx_in[...]
        dg_ref[...] = jnp.zeros_like(dg_ref)

    expert = lead_ref[0] + step
    rows = x_ref.shape[0]
    chunk = min(256, rows)
    for lo in range(0, rows, chunk):
        part = slice(lo, lo + chunk)
        gates = gates_ref[part, :]
        lane = lax.broadcasted_iota(jnp.int32, gates.shape, 1) == expert
        gate = jnp.sum(jnp.where(lane, gates, 0.0), axis=1, keepdims=True)
        both = mm(x_ref[part, :], win_ref[0], NN)
        dh0 = mm(g_ref[part, :], wout_ref[0], NT)
        a = both[:, :FF]
        up = both[:, FF:]
        s = 1.0 / (1.0 + jnp.exp(-a))
        act = a * s
        hid = act * up
        dgate = jnp.sum(hid * dh0, axis=1, keepdims=True)
        dg_ref[part, :] += jnp.where(lane, dgate, 0.0)
        gh = (gate * hid).astype(jnp.bfloat16)
        gh_ref[part, :] = gh
        mix_ref[part, :] += mm(gh, wout_ref[0], NN)
        dh = gate * dh0
        dgu_ref[part, :FF] = (dh * up * (s * (1.0 + a * (1.0 - s)))).astype(jnp.bfloat16)
        dgu_ref[part, FF:] = (dh * act).astype(jnp.bfloat16)
        dx_ref[part, :] += mm(dgu_ref[part, :], win_ref[0], NT)
    width = xt_ref.shape[0]
    for lo in range(0, width, 256):
        part = slice(lo, lo + 256)
        dwin_ref[0, part, :] = mm(xt_ref[part, :], dgu_ref[...], NN).astype(jnp.bfloat16)
    for lo in range(0, FF, 256):
        part = slice(lo, lo + 256)
        dwout_ref[0, part, :] = mm(gh_ref[:, part], g_ref[...], TN).astype(jnp.bfloat16)


def expert_call(lead, x_two, x_turned, cotangent, gates, w_in, w_out, mix, dx):
    rows, width = x_two.shape
    count = w_in.shape[0]
    one = pl.Buffered(1)

    def whole(shape):
        return pl.BlockSpec(shape, lambda e, lead_ref: (0, 0), pipeline_mode=one)

    win_spec = pl.BlockSpec((1,) + w_in.shape[1:], lambda e, lead_ref: (e, 0, 0))
    wout_spec = pl.BlockSpec((1,) + w_out.shape[1:], lambda e, lead_ref: (e, 0, 0))
    full = whole((rows, width))
    return pl.pallas_call(
        expert_kernel,
        grid_spec=pltpu.PrefetchScalarGridSpec(
            num_scalar_prefetch=1,
            grid=(count,),
            in_specs=[
                full, whole((width, rows)), full, whole(gates.shape), win_spec, wout_spec, full, full
            ],
            out_specs=[full, full, whole(gates.shape), win_spec, wout_spec],
            scratch_shapes=[
                pltpu.VMEM((rows, FF), jnp.bfloat16),
                pltpu.VMEM((rows, 2 * FF), jnp.bfloat16),
            ],
        ),
        out_shape=[
            jax.ShapeDtypeStruct(mix.shape, jnp.float32),
            jax.ShapeDtypeStruct(dx.shape, jnp.float32),
            jax.ShapeDtypeStruct(gates.shape, jnp.float32),
            jax.ShapeDtypeStruct(w_in.shape, jnp.bfloat16),
            jax.ShapeDtypeStruct(w_out.shape, jnp.bfloat16),
        ],
        input_output_aliases={7: 0, 8: 1},
        compiler_params=pltpu.CompilerParams(vmem_limit_bytes=58 * 2**20),
        cost_estimate=pl.CostEstimate(
            flops=count * 18 * rows * width * FF,
            bytes_accessed=count * 12 * 2**20 + 24 * 2**20,
            transcendentals=0,
        ),
    )(lead, x_two, x_turned, cotangent, gates, w_in, w_out, mix, dx)


def swap(array, axis, size, bit):
    return lax.ppermute(array, axis, [(i, i ^ bit) for i in range(size)])


def bits_of(size):
    return [1 << b for b in range(size.bit_length() - 1)]


def spread(own, size):
    slots = [own]
    for j in range(1, size):
        low = j & -j
        slots.append(None)
    for bit in reversed(bits_of(size)):
        for j in range(0, size, 2 * bit):
            slots[j + bit] = swap(slots[j], "shard", size, bit)
    return slots


def placed_rows(slots):
    me = lax.axis_index("shard")
    rows = slots[0].shape[0]
    full = jnp.zeros((rows * len(slots), slots[0].shape[1]), slots[0].dtype)
    for j, slot in enumerate(slots):
        full = lax.dynamic_update_slice_in_dim(full, slot, (me ^ j) * rows, 0)
    return full


def halve(piece, size, bit):
    side = (lax.axis_index("rep") // bit) % 2
    half = piece.shape[0] // 2
    keep = lax.dynamic_slice_in_dim(piece, side * half, half, 0)
    give = lax.dynamic_slice_in_dim(piece, (1 - side) * half, half, 0)
    return keep + swap(give, "rep", size, bit)


def rejoin(piece, size, bit):
    side = (lax.axis_index("rep") // bit) % 2
    other = swap(piece, "rep", size, bit)
    first = jnp.where(side == 0, piece, other)
    second = jnp.where(side == 0, other, piece)
    return jnp.concatenate([first, second], axis=0)


def advance(slots, k, n_rep, n_shard):
    folds = bits_of(n_shard // 2)
    rep_bits = bits_of(n_rep)
    slots = list(slots)
    if k < len(folds):
        bit = folds[k]
        for j in range(0, n_shard // 2, 2 * bit):
            slots[j] = slots[j] + swap(slots[j + bit], "shard", n_shard, 2 * bit)
        return slots
    k -= len(folds)
    if k < len(rep_bits):
        return [halve(slots[0], n_rep, rep_bits[k])]
    k -= len(rep_bits)
    return [rejoin(slots[0], n_rep, rep_bits[len(rep_bits) - 1 - k])]


def fold(slots, size):
    slots = list(slots)
    for bit in bits_of(size):
        for j in range(0, size, 2 * bit):
            slots[j] = slots[j] + swap(slots[j + bit], "shard", size, bit)
    return slots[0]


def sum_rep(piece, size):
    me = lax.axis_index("rep")
    for bit in bits_of(size):
        half = piece.shape[0] // 2
        side = (me // bit) % 2
        keep = lax.dynamic_slice_in_dim(piece, side * half, half, 0)
        give = lax.dynamic_slice_in_dim(piece, (1 - side) * half, half, 0)
        piece = keep + swap(give, "rep", size, bit)
    for bit in reversed(bits_of(size)):
        side = (me // bit) % 2
        other = swap(piece, "rep", size, bit)
        first = jnp.where(side == 0, piece, other)
        second = jnp.where(side == 0, other, piece)
        piece = jnp.concatenate([first, second], axis=0)
    return piece


def pack(parts, multiple):
    wide = parts[0].shape[1]
    rows = [parts[0]]
    small = jnp.concatenate([p.reshape(-1) for p in parts[1:]])
    count = -(-small.shape[0] // wide)
    total = -(-(parts[0].shape[0] + count) // multiple) * multiple - parts[0].shape[0]
    small = jnp.pad(small, (0, total * wide - small.shape[0])).reshape(total, wide)
    return jnp.concatenate([parts[0], small], axis=0)


def owned(array, size, slot):
    rows = array.shape[0] // size
    lead = (lax.axis_index("shard") ^ slot) * rows
    return lax.dynamic_slice_in_dim(array, lead, rows, 0).astype(jnp.bfloat16)


def norm_back(d_normed, normed, gain_vec, inverse_rms):
    scaled = d_normed * gain_vec
    return inverse_rms * (scaled - normed * jnp.mean(scaled * normed, axis=1, keepdims=True))


def local(
    n_rep, n_shard,
    tokens, lengths, routes, w_q, w_kv, w_o, w_router, gain_attn, gain_ffn, w_in, w_out, cotangent,
):
    tok_rows = tokens.shape[0]
    kv_width = KV_HEADS * HD
    expert_count = w_in.shape[0] * n_shard
    per_dev = w_in.shape[0]
    is_valid, seq_ids, places = layout(lengths, tok_rows, BLK)
    valid_rows = is_valid.astype(jnp.float32)[:, None]
    key_seq = jnp.where(is_valid > 0, seq_ids, -1)
    own_rows = w_q.shape[0]
    dense = spread(
        pack([jnp.concatenate([w_q, w_kv, w_o], axis=0), w_router, gain_attn, gain_ffn], 16), n_shard
    )
    q_full = placed_rows([d[:own_rows] for d in dense])
    kv_full = placed_rows([d[own_rows : 2 * own_rows] for d in dense])
    o_full = placed_rows([d[2 * own_rows : 3 * own_rows] for d in dense])
    rest = [d[3 * own_rows :].reshape(-1) for d in dense]
    count = own_rows * w_router.shape[1]
    router_full = placed_rows([r[:count].reshape(w_router.shape) for r in rest])
    gain_one = placed_rows([r[count : count + own_rows, None] for r in rest])[:, 0]
    gain_two = placed_rows([r[count + own_rows : count + 2 * own_rows, None] for r in rest])[:, 0]
    w_in, w_out, q_full = lax.optimization_barrier((w_in, w_out, q_full))
    gain_one = gain_one.astype(jnp.float32)[None, :]
    gain_two = gain_two.astype(jnp.float32)[None, :]
    win_slots = spread(w_in, n_shard)
    wout_slots = spread(w_out, n_shard)
    x_float = tokens.astype(jnp.float32)
    scale_one = lax.rsqrt(jnp.mean(x_float * x_float, axis=1, keepdims=True) + epsilon)
    normed_one = x_float * scale_one
    x_one = (normed_one * gain_one).astype(jnp.bfloat16)
    q_lin = jnp.dot(x_one, q_full, preferred_element_type=jnp.float32)
    kv_lin = jnp.dot(x_one, kv_full, preferred_element_type=jnp.float32)
    q_rot = rotate(q_lin, places, HEADS, HD, 1.0).astype(jnp.bfloat16)
    k_rot = rotate(kv_lin[:, :kv_width], places, KV_HEADS, HD, 1.0).astype(jnp.bfloat16)
    v_val = kv_lin[:, kv_width:].astype(jnp.bfloat16)
    attended = attend_forward(q_rot, k_rot, v_val, key_seq)
    branch = jnp.dot(attended, o_full, preferred_element_type=jnp.float32)
    mixed_rows = x_float + valid_rows * branch
    scale_two = lax.rsqrt(jnp.mean(mixed_rows * mixed_rows, axis=1, keepdims=True) + epsilon)
    normed_two = mixed_rows * scale_two
    x_two = (normed_two * gain_two).astype(jnp.bfloat16)
    logits = jnp.dot(x_two, router_full, preferred_element_type=jnp.float32)
    expert_ids = jnp.arange(expert_count, dtype=jnp.int32)
    named = jnp.any(routes[:, :, None] == expert_ids[None, None, :], axis=1)
    top_logit = jnp.max(jnp.where(named, logits, -jnp.inf), axis=1, keepdims=True)
    raised = jnp.where(named, jnp.exp(jnp.where(named, logits - top_logit, 0.0)), 0.0)
    gates = valid_rows * (raised / jnp.sum(raised, axis=1, keepdims=True))
    x_turned = x_two.T
    me = lax.axis_index("shard")
    mix = mixed_rows
    dx = jnp.zeros_like(mixed_rows)
    d_gates = jnp.zeros_like(gates)
    gin_slots = [None] * n_shard
    gout_slots = [None] * n_shard
    for j in range(n_shard):
        lead = ((me ^ j) * per_dev).astype(jnp.int32).reshape(1)
        mix, dx, d_part, gin_slots[j], gout_slots[j] = expert_call(
            lead, x_two, x_turned, cotangent, gates, win_slots[j], wout_slots[j], mix, dx
        )
        d_gates = d_gates + d_part
    layer_out = mix.astype(jnp.bfloat16)
    pieces = []
    low = 1
    gin_fold = list(gin_slots)
    gout_fold = list(gout_slots)
    for j in range(0, n_shard, 2):
        moved_in = swap(gin_slots[j + 1], "shard", n_shard, low)
        moved_out = swap(gout_slots[j + 1], "shard", n_shard, low)
        gin_fold[j] = (gin_slots[j], moved_in)
        gout_fold[j] = (gout_slots[j], moved_out)
    for e in range(per_dev):
        slots = [
            jnp.concatenate(
                [
                    gin_fold[j][0][e] + gin_fold[j][1][e],
                    gout_fold[j][0][e] + gout_fold[j][1][e],
                ],
                axis=0,
            )
            for j in range(0, n_shard, 2)
        ]
        pieces.append(slots)
    held = pieces[0][-1]
    step_count = len(bits_of(n_shard // 2)) + 2 * len(bits_of(n_rep))
    for wave in range(step_count + per_dev - 1):
        for e in range(per_dev):
            if 0 <= wave - e < step_count:
                pieces[e] = advance(pieces[e], wave - e, n_rep, n_shard)
        pieces = lax.optimization_barrier(pieces)
    pieces = [slots[0] for slots in pieces]
    width = w_in.shape[1]
    grad_in = jnp.stack([piece[:width] for piece in pieces]).astype(jnp.float32)
    grad_out = jnp.stack([piece[width:] for piece in pieces]).astype(jnp.float32)

    d_out = cotangent.astype(jnp.float32)
    d_logits = (gates * (d_gates - jnp.sum(gates * d_gates, axis=1, keepdims=True))).astype(
        jnp.bfloat16
    )
    d_router = jnp.einsum("td,te->de", x_two, d_logits, preferred_element_type=jnp.float32)
    d_two = dx + jnp.einsum("te,de->td", d_logits, router_full, preferred_element_type=jnp.float32)
    d_gain_two = jnp.sum(d_two * normed_two, axis=0)
    d_mixed = d_out + norm_back(d_two, normed_two, gain_two, scale_two)
    d_branch = (valid_rows * d_mixed).astype(jnp.bfloat16)
    d_w_o = jnp.einsum("tq,td->qd", attended, d_branch, preferred_element_type=jnp.float32)
    d_attended = jnp.einsum(
        "td,qd->tq", d_branch, o_full, preferred_element_type=jnp.float32
    ).astype(jnp.bfloat16)
    early = sum_rep(
        fold(
            [
                pack(
                    [
                        owned(d_w_o, n_shard, j),
                        owned(d_router, n_shard, j),
                        owned(d_gain_two, n_shard, j),
                    ],
                    16 * n_rep,
                )
                for j in range(n_shard)
            ],
            n_shard,
        ),
        n_rep,
    )
    d_query, d_keys, d_vals = attend_backward(q_rot, k_rot, v_val, d_attended, key_seq, held)
    d_q_lin = rotate(d_query, places, HEADS, HD, -1.0).astype(jnp.bfloat16)
    d_kv_lin = jnp.concatenate([rotate(d_keys, places, KV_HEADS, HD, -1.0), d_vals], axis=1).astype(
        jnp.bfloat16
    )
    d_w_q = jnp.einsum("td,tq->dq", x_one, d_q_lin, preferred_element_type=jnp.float32)
    d_w_kv = jnp.einsum("td,tq->dq", x_one, d_kv_lin, preferred_element_type=jnp.float32)
    d_one = jnp.einsum(
        "tq,dq->td", d_q_lin, q_full, preferred_element_type=jnp.float32
    ) + jnp.einsum("tq,dq->td", d_kv_lin, kv_full, preferred_element_type=jnp.float32)
    d_gain_one = jnp.sum(d_one * normed_one, axis=0)
    d_tokens = (d_mixed + norm_back(d_one, normed_one, gain_one, scale_one)).astype(jnp.bfloat16)
    late = sum_rep(
        fold(
            [
                pack(
                    [
                        jnp.concatenate([owned(d_w_q, n_shard, j), owned(d_w_kv, n_shard, j)], axis=0),
                        owned(d_gain_one, n_shard, j),
                    ],
                    16,
                )
                for j in range(n_shard)
            ],
            n_shard,
        ),
        n_rep,
    )
    small = early[own_rows:].reshape(-1).astype(jnp.float32)
    router_size = own_rows * expert_count
    return (
        layer_out,
        d_tokens,
        late[:own_rows].astype(jnp.float32),
        late[own_rows : 2 * own_rows].astype(jnp.float32),
        early[:own_rows].astype(jnp.float32),
        small[:router_size].reshape(own_rows, expert_count),
        late[2 * own_rows :].reshape(-1)[:own_rows].astype(jnp.float32),
        small[router_size : router_size + own_rows],
        grad_in,
        grad_out,
    )


def solution(mesh):
    placed = (
        P(("rep", "shard"), None),
        P(("rep", "shard"), None),
        P(("rep", "shard"), None),
        P("shard", None),
        P("shard", None),
        P("shard", None),
        P("shard", None),
        P("shard"),
        P("shard"),
        P("shard", None, None),
        P("shard", None, None),
        P(("rep", "shard"), None),
    )
    return jax.shard_map(
        functools.partial(local, mesh.shape["rep"], mesh.shape["shard"]),
        mesh=mesh,
        in_specs=placed,
        out_specs=(
            P(("rep", "shard"), None),
            P(("rep", "shard"), None),
            P("shard", None),
            P("shard", None),
            P("shard", None),
            P("shard", None),
            P("shard"),
            P("shard"),
            P("shard", None, None),
            P("shard", None, None),
        ),
        check_vma=False,
    )
```
